128 devices in a mesh: pair: 32 (over z, y, x_hi), rows: 4 (over x_lo, core).
Axes of the slice: x: 4 (x_hi: 2, x_lo: 2; x = x_hi * 2 + x_lo), y: 4, z: 4, core: 2. Of those that a mesh axis runs over, the one named last changes fastest.
Arguments:
- matrix: float32 [16384, 16384], P('rows', 'pair')
Outputs:
- rotated: float32 [16384, 16384], P('rows', 'pair')
All inputs are finite; a program needn't handle non-finite values.
Results may differ from the reference program's by a relative error of at most 0.00016.
Values sent between devices are 32-bit elements; how exact they have to be, the bound alone decides.
No kernel may reach another device: no remote copies, remote signals or barrier semaphores. Data moves between devices by JAX's collectives and lax.ppermute only.
A program may use at most 128 MiB of HBM per device.

```python
import jax
import jax.numpy as jnp
from jax import lax

B = 64
ROUNDS = 3
NS_STEPS = 8
W = 128
NPAIRS = 128
N = 16384
M = 16384


def draw_matrix(key, part):
    key = jax.random.fold_in(key, 7)
    key_noise, key_row, key_col, key_scale = jax.random.split(key, 4)
    noise = jax.random.normal(key_noise, (M, N), jnp.float32)
    row_part = jax.random.normal(key_row, (M, 1), jnp.float32)
    log_scale = jax.random.uniform(key_scale, (1, N), jnp.float32, jnp.log(0.5), jnp.log(5.0))
    col_part = jax.random.normal(key_col, (1, N), jnp.float32)
    values = (noise + row_part * col_part) * jnp.exp(log_scale)
    return jnp.clip(values, -60.0, 60.0).astype(jnp.float32)


def setup_inputs(seed: int = 0) -> dict:
    streams_of = jax.random.split(jax.random.key(seed), 2)
    return {
        "matrix": draw_matrix(jax.random.fold_in(streams_of[1], 71), 0),
    }


EPS = 1e-06

def rotation_factors(gram):
    diag = jnp.diagonal(gram, axis1=-2, axis2=-1)
    norms = jnp.sqrt(diag + EPS)
    corr = gram / (norms[..., :, None] * norms[..., None, :])
    upper = jnp.triu(corr, 1)
    skew = 0.5 * (jnp.swapaxes(upper, -1, -2) - upper)
    total = lax.optimization_barrier(jnp.sum(skew * skew, axis=(-2, -1), keepdims=True))
    eye = jnp.eye(gram.shape[-1], dtype=jnp.float32)
    current = (eye + skew) / jnp.sqrt(1.0 + total)
    for step in range(NS_STEPS):
        inner = jnp.einsum('pki,pkj->pij', current, current, precision=lax.Precision.HIGHEST)
        current = 1.5 * current - 0.5 * jnp.einsum('pik,pkj->pij', current, inner, precision=lax.Precision.HIGHEST)
    return current

def reference(matrix):
    rows_all = matrix.shape[0]
    work = matrix.reshape(rows_all, NPAIRS, W)
    for step in range(ROUNDS):
        gram = jnp.einsum('rpi,rpj->pij', work, work, precision=lax.Precision.HIGHEST)
        factors = rotation_factors(gram)
        work = jnp.einsum('rpi,pij->rpj', work, factors, precision=lax.Precision.HIGHEST)
        tops = work[:, :, :B]
        bottoms = work[:, :, B:]
        new_tops = jnp.concatenate([tops[:, :1], bottoms[:, :1], tops[:, 1:NPAIRS - 1]], axis=1)
        new_bottoms = jnp.concatenate([bottoms[:, 1:], tops[:, NPAIRS - 1:]], axis=1)
        work = jnp.concatenate([new_tops, new_bottoms], axis=2)
    return work.reshape(rows_all, NPAIRS * W)
```

```python
import functools

import jax
import jax.numpy as jnp
from jax import lax
from jax.experimental import pallas as pl
from jax.experimental.pallas import tpu as pltpu
from jax.sharding import PartitionSpec as P

B = 64
W = 128
PD = 4
NS_STEPS = 8
EPS = 1e-06
F32 = jnp.float32
BF16 = jnp.bfloat16

TINY = pl.CostEstimate(flops=1, bytes_accessed=1, transcendentals=0)

NN = (((1,), (0,)), ((), ()))
NT = (((1,), (1,)), ((), ()))
TN = (((0,), (0,)), ((), ()))


def params(mib=48):
    return pltpu.CompilerParams(vmem_limit_bytes=mib * 1024 * 1024)


def split(x):
    high = x.astype(BF16)
    return high, (x - high.astype(F32)).astype(BF16)


def dot(a, b, dims):
    return lax.dot_general(a, b, dims, preferred_element_type=F32)


def factor_stack(y):
    high, low = split(y)
    return jnp.concatenate(
        [jnp.concatenate([high, high], 1), jnp.concatenate([low, jnp.zeros_like(low)], 1)], 0
    )


def apply_rows(stack, values):
    high, low = split(values)
    both = dot(stack, jnp.concatenate([high, low], 0), NN)
    half = both.shape[0] // 2
    return both[:half] + both[half:]


def finish_gram(acc):
    cross = acc[:, W:]
    return acc[:, :W] + cross + cross.T


def gram_rows_kernel(m_ref, g_ref, acc):
    step = pl.program_id(0)

    @pl.when(step == 0)
    def _():
        acc[...] = jnp.zeros_like(acc)

    for k in range(PD):
        high, low = split(m_ref[:, k * W : (k + 1) * W])
        acc[k] += dot(high, jnp.concatenate([high, low], 1), TN)

    @pl.when(step == pl.num_programs(0) - 1)
    def _():
        for k in range(PD):
            g_ref[k] = finish_gram(acc[k])


def gram_rows(matrix, chunk=512):
    rows = matrix.shape[0]
    return pl.pallas_call(
        gram_rows_kernel,
        grid=(rows // chunk,),
        in_specs=[pl.BlockSpec((chunk, PD * W), lambda i: (i, 0))],
        out_specs=pl.BlockSpec((PD, W, W), lambda i: (0, 0, 0)),
        out_shape=jax.ShapeDtypeStruct((PD, W, W), F32),
        scratch_shapes=[pltpu.VMEM((PD, W, 2 * W), F32)],
        compiler_params=params(),
        cost_estimate=TINY,
        name="gram_rows",
    )(matrix)


def gram_blocks_kernel(n, *refs):
    acc = refs[-1]
    g_ref = refs[-2]
    step = pl.program_id(0)

    @pl.when(step == 0)
    def _():
        acc[...] = jnp.zeros_like(acc)

    for k in range(n):
        high, low = split(jnp.concatenate([refs[2 * k][...], refs[2 * k + 1][...]], 0))
        acc[k] += dot(high, jnp.concatenate([high, low], 0), NT)

    @pl.when(step == pl.num_programs(0) - 1)
    def _():
        for k in range(n):
            g_ref[k] = finish_gram(acc[k])


def gram_blocks(pairs, name, chunk=1024):
    blocks = [x for pair in pairs for x in pair]
    n = len(pairs)
    cols = blocks[0].shape[1]
    return pl.pallas_call(
        functools.partial(gram_blocks_kernel, n),
        grid=(cols // chunk,),
        in_specs=[pl.BlockSpec((B, chunk), lambda i: (0, i))] * (2 * n),
        out_specs=pl.BlockSpec((n, W, W), lambda i: (0, 0, 0)),
        out_shape=jax.ShapeDtypeStruct((n, W, W), F32),
        scratch_shapes=[pltpu.VMEM((n, W, 2 * W), F32)],
        compiler_params=params(),
        cost_estimate=TINY,
        name=name,
    )(*blocks)


def mm3(a, b, dims):
    ah, al = split(a)
    bh, bl = split(b)
    return dot(ah, bh, dims) + (dot(ah, bl, dims) + dot(al, bh, dims))


def factors_kernel(n, swapped, flags, a_ref, b_ref, y_ref):
    row = lax.broadcasted_iota(jnp.int32, (W, W), 0)
    col = lax.broadcasted_iota(jnp.int32, (W, W), 1)
    eye = row == col
    ys = []
    for k in range(n):
        g = a_ref[k] + b_ref[k]
        diag = jnp.where(eye, g, 0.0)
        norm_col = jnp.sqrt(jnp.sum(diag, axis=1, keepdims=True) + EPS)
        norm_row = jnp.sqrt(jnp.sum(diag, axis=0, keepdims=True) + EPS)
        corr = g / (norm_col * norm_row)
        skew = jnp.where(row < col, -0.5 * corr, jnp.where(row > col, 0.5 * corr, 0.0))
        total = jnp.sum(jnp.sum(skew * skew, axis=1, keepdims=True), axis=0, keepdims=True)
        ys.append((jnp.where(eye, 1.0, 0.0) - skew) / jnp.sqrt(1.0 + total))

    def step(_, ys):
        inner = [mm3(y, y, NT) for y in ys]
        return tuple(1.5 * y - 0.5 * mm3(a, y, NN) for a, y in zip(inner, ys))

    ys = lax.fori_loop(0, NS_STEPS, step, tuple(ys))
    for k in range(n):
        y = ys[k]
        if k == swapped:
            y = jnp.where(flags[0] != 0, jnp.concatenate([y[B:], y[:B]], 0), y)
        y_ref[k] = y


def factors(flags, a, b, name, swapped=0):
    n = a.shape[0]
    return pl.pallas_call(
        functools.partial(factors_kernel, n, swapped),
        in_specs=[
            pl.BlockSpec(memory_space=pltpu.SMEM),
            pl.BlockSpec(memory_space=pltpu.VMEM),
            pl.BlockSpec(memory_space=pltpu.VMEM),
        ],
        out_specs=pl.BlockSpec(memory_space=pltpu.VMEM),
        out_shape=jax.ShapeDtypeStruct((n, W, W), F32),
        compiler_params=params(),
        cost_estimate=TINY,
        name=name,
    )(flags, a, b)


def rotate_rows_kernel(y_ref, m_ref, *outs):
    for k in range(PD):
        stack = factor_stack(y_ref[k])
        high, low = split(m_ref[:, k * W : (k + 1) * W])
        both = dot(stack, jnp.concatenate([high, low], 1), NT)
        new = both[:W] + both[W:]
        outs[2 * k][...] = new[:B]
        outs[2 * k + 1][...] = new[B:]


def rotate_rows(y, matrix, chunk=512):
    rows = matrix.shape[0]
    outs = pl.pallas_call(
        rotate_rows_kernel,
        grid=(rows // chunk,),
        in_specs=[
            pl.BlockSpec((PD, W, W), lambda i: (0, 0, 0)),
            pl.BlockSpec((chunk, PD * W), lambda i: (i, 0)),
        ],
        out_specs=[pl.BlockSpec((B, chunk), lambda i: (0, i))] * (2 * PD),
        out_shape=[jax.ShapeDtypeStruct((B, rows), F32)] * (2 * PD),
        compiler_params=params(),
        cost_estimate=TINY,
        name="rotate_rows",
    )(y, matrix)
    return [outs[2 * k] for k in range(PD)], [outs[2 * k + 1] for k in range(PD)]


def rotate_blocks_kernel(n, *refs):
    y_ref = refs[0]
    ins, outs = refs[1 : 1 + 2 * n], refs[1 + 2 * n :]
    for k in range(n):
        new = apply_rows(
            factor_stack(y_ref[k]), jnp.concatenate([ins[2 * k][...], ins[2 * k + 1][...]], 0)
        )
        outs[2 * k][...] = new[:B]
        outs[2 * k + 1][...] = new[B:]


def rotate_blocks(y, pairs, name, chunk=1024):
    blocks = [x for pair in pairs for x in pair]
    n = len(pairs)
    cols = blocks[0].shape[1]
    spec = pl.BlockSpec((B, chunk), lambda i: (0, i))
    outs = pl.pallas_call(
        functools.partial(rotate_blocks_kernel, n),
        grid=(cols // chunk,),
        in_specs=[pl.BlockSpec((n, W, W), lambda i: (0, 0, 0))] + [spec] * (2 * n),
        out_specs=[spec] * (2 * n),
        out_shape=[jax.ShapeDtypeStruct((B, cols), F32)] * (2 * n),
        compiler_params=params(),
        cost_estimate=TINY,
        name=name,
    )(y, *blocks)
    return [outs[2 * k] for k in range(n)], [outs[2 * k + 1] for k in range(n)]


def rotate_ends_kernel(flags, yl_ref, yr_ref, lt, lb, rt, rb, l_edge, r_edge, left, right):
    new = apply_rows(factor_stack(yl_ref[...]), jnp.concatenate([lt[...], lb[...]], 0))
    left[...] = jnp.where(flags[0] != 0, l_edge[...], new)
    new = apply_rows(factor_stack(yr_ref[...]), jnp.concatenate([rt[...], rb[...]], 0))
    right[...] = jnp.where(flags[1] != 0, r_edge[...], new)


def rotate_ends(flags, y_left, y_right, left_pair, right_pair, edges, name, chunk=1024):
    cols = edges[0].shape[1]
    spec = pl.BlockSpec((B, chunk), lambda i: (0, i))
    half = pl.BlockSpec((B, W), lambda i: (0, 0))
    return pl.pallas_call(
        rotate_ends_kernel,
        grid=(cols // chunk,),
        in_specs=[pl.BlockSpec(memory_space=pltpu.SMEM), half, half] + [spec] * 6,
        out_specs=[spec] * 2,
        out_shape=[jax.ShapeDtypeStruct((B, cols), F32)] * 2,
        compiler_params=params(),
        cost_estimate=TINY,
        name=name,
    )(flags, y_left, y_right, *left_pair, *right_pair, *edges)


def final_kernel(flags, y_ref, yl_ref, yr_ref, *refs):
    out = refs[-1]
    values = [jnp.concatenate([refs[2 * k][...], refs[2 * k + 1][...]], 0) for k in range(PD + 2)]
    own = [
        apply_rows(factor_stack(y_ref[k]), values[k + 1]) for k in range(PD)
    ]
    left = apply_rows(factor_stack(yl_ref[...]), values[0])
    right = apply_rows(factor_stack(yr_ref[...]), values[PD + 1])
    left = jnp.where(flags[0] != 0, own[0][B:], left)
    right = jnp.where(flags[1] != 0, own[PD - 1][:B], right)
    tops = [left] + [x[:B] for x in own[: PD - 1]]
    bottoms = [x[B:] for x in own[1:]] + [right]
    for k in range(PD):
        out[:, k * W : (k + 1) * W] = jnp.concatenate([tops[k], bottoms[k]], 0).T


def final(flags, y, y_left, y_right, pairs, chunk=512):
    blocks = [x for pair in pairs for x in pair]
    cols = blocks[0].shape[1]
    spec = pl.BlockSpec((B, chunk), lambda i: (0, i))
    half = pl.BlockSpec((B, W), lambda i: (0, 0))
    return pl.pallas_call(
        final_kernel,
        grid=(cols // chunk,),
        in_specs=[
            pl.BlockSpec(memory_space=pltpu.SMEM),
            pl.BlockSpec((PD, W, W), lambda i: (0, 0, 0)),
            half,
            half,
        ]
        + [spec] * len(blocks),
        out_specs=pl.BlockSpec((chunk, PD * W), lambda i: (i, 0)),
        out_shape=jax.ShapeDtypeStruct((cols, PD * W), F32),
        compiler_params=params(),
        cost_estimate=TINY,
        name="final",
    )(flags, y, y_left, y_right, *blocks)


def send_on(x):
    peers = lax.axis_size("pair")
    return lax.ppermute(x, "pair", [(i, i + 1) for i in range(peers - 1)])


def send_back(x):
    peers = lax.axis_size("pair")
    return lax.ppermute(x, "pair", [(i + 1, i) for i in range(peers - 1)])


def row_terms(gram):
    near = gram + lax.ppermute(gram, "rows", [(i, i ^ 1) for i in range(4)])
    return near, lax.ppermute(near, "rows", [(i, i ^ 2) for i in range(4)])


def body(matrix):
    index = lax.axis_index("pair")
    last = lax.axis_size("pair") - 1
    first_one, last_one = index == 0, index == last
    flags = jnp.stack([first_one, last_one]).astype(jnp.int32)

    y1 = factors(flags, *row_terms(gram_rows(matrix)), name="factors_1")
    r1, l1 = rotate_rows(y1, matrix)

    in_left = send_on(r1[3])
    in_right = send_back(l1[0])
    in_left2 = send_on(r1[2])
    in_right2 = send_back(l1[1])

    in_left = jnp.where(first_one, l1[0], in_left)
    in_right = jnp.where(last_one, r1[3], in_right)
    inner2 = [(r1[0], l1[2]), (r1[1], l1[3])]
    outer2 = [(in_left, l1[1]), (r1[2], in_right)]
    g2_inner = gram_blocks(inner2, "gram_2_inner")
    y2_inner = factors(flags, *row_terms(g2_inner), name="factors_2_inner", swapped=-1)
    (r2_1, r2_2), (l2_1, l2_2) = rotate_blocks(y2_inner, inner2, "rotate_2_inner")
    in_left3 = send_on(r2_2)
    in_right3 = send_back(l2_1)

    g2_outer = gram_blocks(outer2, "gram_2_outer")
    y2_outer = factors(flags, *row_terms(g2_outer), name="factors_2_outer")
    y2_left = send_on(y2_outer[1, :B])
    y2_right = send_back(y2_outer[0, B:])
    (r2_0, r2_3), (l2_0, l2_3) = rotate_blocks(y2_outer, outer2, "rotate_2_outer")

    inner3 = [(r2_0, l2_2), (r2_1, l2_3)]
    g3_inner = gram_blocks(inner3, "gram_3_inner")
    y3_inner = factors(flags, *row_terms(g3_inner), name="factors_3_inner", swapped=-1)

    r2_left, l2_right = rotate_ends(
        flags, y2_left, y2_right, (in_left2, l1[0]), (r1[3], in_right2), (l2_0, r2_3), "ends_2"
    )
    outer3 = [(r2_left, l2_1), (r2_2, l2_right)]
    g3_outer = gram_blocks(outer3, "gram_3_outer")
    y3_outer = factors(flags, *row_terms(g3_outer), name="factors_3_outer")
    y3_left = send_on(y3_outer[1, :B])
    y3_right = send_back(y3_outer[0, B:])

    y3 = jnp.stack([y3_outer[0], y3_inner[0], y3_inner[1], y3_outer[1]])
    pairs = [(in_left3, l2_0), outer3[0], inner3[0], inner3[1], outer3[1], (r2_3, in_right3)]
    return final(flags, y3, y3_left, y3_right, pairs)


def solution(mesh):
    spec = P("rows", "pair")
    return jax.shard_map(body, mesh=mesh, in_specs=(spec,), out_specs=spec, check_vma=False)
```

```python
import functools

import jax
import jax.numpy as jnp
from jax import lax
from jax.experimental import pallas as pl
from jax.experimental.pallas import tpu as pltpu
from jax.sharding import PartitionSpec as P

B = 64
W = 128
PD = 4
NS_STEPS = 8
EPS = 1e-06
F32 = jnp.float32
BF16 = jnp.bfloat16

LONG = pl.CostEstimate(flops=10**10, bytes_accessed=4 * 10**8, transcendentals=0)

NN = (((1,), (0,)), ((), ()))
NT = (((1,), (1,)), ((), ()))
TN = (((0,), (0,)), ((), ()))


def params(mib=60):
    return pltpu.CompilerParams(vmem_limit_bytes=mib * 1024 * 1024)


def split(x):
    high = x.astype(BF16)
    return high, (x - high.astype(F32)).astype(BF16)


def dot(a, b, dims):
    return lax.dot_general(a, b, dims, preferred_element_type=F32)


def factor_stack(y):
    high, low = split(y)
    return jnp.concatenate(
        [jnp.concatenate([high, high], 1), jnp.concatenate([low, jnp.zeros_like(low)], 1)], 0
    )


def apply_rows(stack, values):
    high, low = split(values)
    both = dot(stack, jnp.concatenate([high, low], 0), NN)
    half = both.shape[0] // 2
    return both[:half] + both[half:]


def finish_gram(acc):
    cross = acc[:, W:]
    return acc[:, :W] + cross + cross.T


def store_gram(flags, acc, mine, theirs):
    half = PD // 2
    core = flags[2]
    for j in range(half):
        mine[j] = finish_gram(acc[core * half + j])
        theirs[j] = finish_gram(acc[(1 - core) * half + j])


def gram_rows_kernel(flags, *refs):
    cols, (mine, theirs, acc) = refs[:PD], refs[PD:]
    step = pl.program_id(0)

    @pl.when(step == 0)
    def _():
        acc[...] = jnp.zeros_like(acc)

    for k in range(PD):
        high, low = split(cols[k][...])
        acc[k] += dot(high, jnp.concatenate([high, low], 1), TN)

    @pl.when(step == pl.num_programs(0) - 1)
    def _():
        store_gram(flags, acc, mine, theirs)


def gram_blocks_kernel(flags, *refs):
    blocks, (grams, acc) = refs[: 2 * PD], refs[2 * PD :]
    step = pl.program_id(0)

    @pl.when(step == 0)
    def _():
        acc[...] = jnp.zeros_like(acc)

    for k in range(PD):
        high, low = split(jnp.concatenate([blocks[2 * k][...], blocks[2 * k + 1][...]], 0))
        acc[k] += dot(high, jnp.concatenate([high, low], 0), NT)

    @pl.when(step == pl.num_programs(0) - 1)
    def _():
        for k in range(PD):
            grams[k] = finish_gram(acc[k])


SMEM_SPEC = pl.BlockSpec(memory_space=pltpu.SMEM)
ANY_SPEC = pl.BlockSpec(memory_space=pl.ANY)


def gram_call(kernel, flags, operands, specs, steps, counts, name):
    return pl.pallas_call(
        kernel,
        grid=(steps,),
        in_specs=[SMEM_SPEC] + specs,
        out_specs=[pl.BlockSpec((n, W, W), lambda i: (0, 0, 0)) for n in counts],
        out_shape=[jax.ShapeDtypeStruct((n, W, W), F32) for n in counts],
        scratch_shapes=[pltpu.VMEM((PD, W, 2 * W), F32)],
        compiler_params=params(),
        cost_estimate=LONG,
        name=name,
    )(flags, *operands)


def column_spec(k, chunk):
    return pl.BlockSpec((chunk, W), lambda i: (i, k))


def gram_rows(flags, matrix, name, chunk=1024):
    specs = [column_spec(k, chunk) for k in range(PD)]
    steps, counts = matrix.shape[0] // chunk, (PD // 2, PD // 2)
    return gram_call(gram_rows_kernel, flags, [matrix] * PD, specs, steps, counts, name)


def gram_blocks(flags, pairs, name, chunk=1024):
    blocks = [x for pair in pairs for x in pair]
    specs = [pl.BlockSpec((B, chunk), lambda i: (0, i))] * len(blocks)
    steps = blocks[0].shape[1] // chunk
    return gram_call(gram_blocks_kernel, flags, blocks, specs, steps, (PD,), name)[0]


def mm3(a, b, dims):
    ah, al = split(a)
    bh, bl = split(b)
    zero = jnp.zeros_like(bl)
    if dims == NT:
        right = jnp.concatenate([jnp.concatenate([bh, bh], 1), jnp.concatenate([bl, zero], 1)], 0)
    else:
        right = jnp.concatenate([jnp.concatenate([bh, bl], 1), jnp.concatenate([bh, zero], 1)], 0)
    out = dot(jnp.concatenate([ah, al], 1), right, dims)
    return out[:, :W] + out[:, W:]


def factors_kernel(flags, a_ref, b_ref, y_ref, *edges):
    row = lax.broadcasted_iota(jnp.int32, (W, W), 0)
    col = lax.broadcasted_iota(jnp.int32, (W, W), 1)
    eye = row == col
    n = y_ref.shape[0]
    ys = []
    for k in range(n):
        g = a_ref[k] + b_ref[k]
        diag = jnp.where(eye, g, 0.0)
        norm_col = jnp.sqrt(jnp.sum(diag, axis=1, keepdims=True) + EPS)
        norm_row = jnp.sqrt(jnp.sum(diag, axis=0, keepdims=True) + EPS)
        corr = g / (norm_col * norm_row)
        skew = jnp.where(row < col, -0.5 * corr, jnp.where(row > col, 0.5 * corr, 0.0))
        total = jnp.sum(jnp.sum(skew * skew, axis=1, keepdims=True), axis=0, keepdims=True)
        ys.append((jnp.where(eye, 1.0, 0.0) - skew) / jnp.sqrt(1.0 + total))

    def step(_, ys):
        inner = [mm3(y, y, NT) for y in ys]
        return tuple(1.5 * y - 0.5 * mm3(a, y, NN) for a, y in zip(inner, ys))

    ys = list(lax.fori_loop(0, NS_STEPS, step, tuple(ys)))
    swap = flags[0] != 0
    if n < PD:
        swap = jnp.logical_and(swap, flags[2] == 0)
    ys[0] = jnp.where(swap, jnp.concatenate([ys[0][B:], ys[0][:B]], 0), ys[0])
    for k in range(n):
        y_ref[k] = ys[k]
    if edges:
        edges[0][...] = ys[0][B:]
        edges[1][...] = ys[n - 1][:B]


def factors(flags, a, b, name):
    vmem = pl.BlockSpec(memory_space=pltpu.VMEM)
    edges = 2 if a.shape[0] == PD else 0
    return pl.pallas_call(
        factors_kernel,
        in_specs=[SMEM_SPEC, vmem, vmem],
        out_specs=[vmem] * (1 + edges),
        out_shape=[jax.ShapeDtypeStruct(a.shape, F32)] + [jax.ShapeDtypeStruct((B, W), F32)] * edges,
        compiler_params=params(),
        cost_estimate=LONG,
        name=name,
    )(flags, a, b)


def factor_of(flags, ys, k, half=None):
    if len(ys) == 1:
        y = ys[0][k]
    else:
        core, slot = divmod(k, PD // 2)
        y = jnp.where(flags[2] == core, ys[0][slot], ys[1][slot])
    return y if half is None else y[half * B : (half + 1) * B]


def rotate_kernel(parts, by_rows, sources, deps, flags, *refs):
    per = 1 if by_rows else 2
    ys, refs = refs[:sources], refs[sources:]
    ins, outs = refs[: per * len(parts)], list(refs[per * len(parts) + deps :])
    for at, (k, half) in enumerate(parts):
        y = factor_of(flags, ys, k, half)
        count = y.shape[0]
        if by_rows:
            high, low = split(ins[at][...])
            both = dot(factor_stack(y), jnp.concatenate([high, low], 1), NT)
            new = both[:count] + both[count:]
        else:
            new = apply_rows(
                factor_stack(y), jnp.concatenate([ins[2 * at][...], ins[2 * at + 1][...]], 0)
            )
        for start in range(0, count, B):
            outs.pop(0)[...] = new[start : start + B]


def rotate_call(flags, ys, parts, by_rows, operands, specs, cols, chunk, name, deps=()):
    count = sum(2 if half is None else 1 for _, half in parts)
    whole = pl.BlockSpec(ys[0].shape, lambda i: (0, 0, 0))
    return pl.pallas_call(
        functools.partial(rotate_kernel, parts, by_rows, len(ys), len(deps)),
        grid=(cols // chunk,),
        in_specs=[SMEM_SPEC] + [whole] * len(ys) + specs + [ANY_SPEC] * len(deps),
        out_specs=[pl.BlockSpec((B, chunk), lambda i: (0, i))] * count,
        out_shape=[jax.ShapeDtypeStruct((B, cols), F32)] * count,
        compiler_params=params(),
        cost_estimate=LONG,
        name=name,
    )(flags, *ys, *operands, *deps)


def rotate_rows(flags, ys, parts, matrix, name, chunk=1024):
    specs = [column_spec(k, chunk) for k, _ in parts]
    operands = [matrix] * len(parts)
    return rotate_call(flags, ys, parts, True, operands, specs, matrix.shape[0], chunk, name)


def rotate_blocks(flags, ys, parts, pairs, name, deps=(), chunk=1024):
    blocks = [x for k, _ in parts for x in pairs[k]]
    specs = [pl.BlockSpec((B, chunk), lambda i: (0, i))] * len(blocks)
    cols = blocks[0].shape[1]
    return rotate_call(flags, ys, parts, False, blocks, specs, cols, chunk, name, deps)


def rotate_ends_kernel(flags, y_left, y_right, lt, lb, rt, rb, l_edge, r_edge, left, right):
    new = apply_rows(factor_stack(y_left[...]), jnp.concatenate([lt[...], lb[...]], 0))
    left[...] = jnp.where(flags[0] != 0, l_edge[...], new)
    new = apply_rows(factor_stack(y_right[...]), jnp.concatenate([rt[...], rb[...]], 0))
    right[...] = jnp.where(flags[1] != 0, r_edge[...], new)


def rotate_ends(flags, edges, left_pair, right_pair, instead, name, chunk=1024):
    cols = instead[0].shape[1]
    spec = pl.BlockSpec((B, chunk), lambda i: (0, i))
    half = pl.BlockSpec((B, W), lambda i: (0, 0))
    return pl.pallas_call(
        rotate_ends_kernel,
        grid=(cols // chunk,),
        in_specs=[SMEM_SPEC, half, half] + [spec] * 6,
        out_specs=[spec] * 2,
        out_shape=[jax.ShapeDtypeStruct((B, cols), F32)] * 2,
        compiler_params=params(),
        cost_estimate=LONG,
        name=name,
    )(flags, *edges, *left_pair, *right_pair, *instead)


def final_inner_kernel(flags, y_ref, *refs):
    ins = refs[: 2 * PD]
    out, l_1, r_2, l_0, r_3 = refs[2 * PD :]

    def rotated(k, half):
        values = jnp.concatenate([ins[2 * k][...], ins[2 * k + 1][...]], 0)
        return apply_rows(factor_stack(factor_of(flags, (y_ref,), k, half)), values)

    own1, own2 = rotated(1, None), rotated(2, None)
    l_1[...] = own1[B:]
    r_2[...] = own2[:B]
    out[:, :W] = jnp.concatenate([rotated(0, 0), own2[B:]], 0).T
    out[:, W:] = jnp.concatenate([own1[:B], rotated(3, 1)], 0).T

    @pl.when(flags[0] != 0)
    def _():
        l_0[...] = rotated(0, 1)

    @pl.when(flags[1] != 0)
    def _():
        r_3[...] = rotated(3, 0)


def edge_specs(chunk):
    return [
        pl.BlockSpec((B, chunk), lambda i, flags: (0, i * flags[0])),
        pl.BlockSpec((B, chunk), lambda i, flags: (0, i * flags[1])),
    ]


def final_inner(flags, y, pairs, chunk=1024):
    blocks = [x for pair in pairs for x in pair]
    cols = blocks[0].shape[1]
    spec = pl.BlockSpec((B, chunk), lambda i, flags: (0, i))
    block = jax.ShapeDtypeStruct((B, cols), F32)
    whole = pl.BlockSpec((PD, W, W), lambda i, flags: (0, 0, 0))
    return pl.pallas_call(
        final_inner_kernel,
        grid_spec=pltpu.PrefetchScalarGridSpec(
            num_scalar_prefetch=1,
            grid=(cols // chunk,),
            in_specs=[whole] + [spec] * len(blocks),
            out_specs=[pl.BlockSpec((chunk, 2 * W), lambda i, flags: (i, 0)), spec, spec]
            + edge_specs(chunk),
        ),
        out_shape=[jax.ShapeDtypeStruct((cols, 2 * W), F32)] + [block] * 4,
        compiler_params=params(),
        cost_estimate=LONG,
        name="final_inner",
    )(flags, y, *blocks)


def final_kernel(flags, y_left, y_right, lt, lb, rt, rb, l_1, r_2, l_0, r_3, inner, out):
    left = apply_rows(factor_stack(y_left[...]), jnp.concatenate([lt[...], lb[...]], 0))
    right = apply_rows(factor_stack(y_right[...]), jnp.concatenate([rt[...], rb[...]], 0))
    left = jnp.where(flags[0] != 0, l_0[...], left)
    right = jnp.where(flags[1] != 0, r_3[...], right)
    out[:, :W] = jnp.concatenate([left, l_1[...]], 0).T
    out[:, W : 3 * W] = inner[...]
    out[:, 3 * W :] = jnp.concatenate([r_2[...], right], 0).T


def final(flags, edges, left_pair, right_pair, done, inner, chunk=1024):
    cols = inner.shape[0]
    spec = pl.BlockSpec((B, chunk), lambda i, flags: (0, i))
    half = pl.BlockSpec((B, W), lambda i, flags: (0, 0))
    return pl.pallas_call(
        final_kernel,
        grid_spec=pltpu.PrefetchScalarGridSpec(
            num_scalar_prefetch=1,
            grid=(cols // chunk,),
            in_specs=[half, half]
            + [spec] * 6
            + edge_specs(chunk)
            + [pl.BlockSpec((chunk, 2 * W), lambda i, flags: (i, 0))],
            out_specs=pl.BlockSpec((chunk, PD * W), lambda i, flags: (i, 0)),
        ),
        out_shape=jax.ShapeDtypeStruct((cols, PD * W), F32),
        compiler_params=params(),
        cost_estimate=LONG,
        name="final",
    )(flags, *edges, *left_pair, *right_pair, *done, inner)


def send_on(x):
    peers = lax.axis_size("pair")
    return lax.ppermute(x, "pair", [(i, i + 1) for i in range(peers - 1)])


def send_back(x):
    peers = lax.axis_size("pair")
    return lax.ppermute(x, "pair", [(i + 1, i) for i in range(peers - 1)])


def after(x, *deps):
    return pl.pallas_call(
        lambda *refs: None,
        in_specs=[pl.BlockSpec(memory_space=pl.ANY)] * (1 + len(deps)),
        out_specs=pl.BlockSpec(memory_space=pl.ANY),
        out_shape=jax.ShapeDtypeStruct(x.shape, x.dtype),
        input_output_aliases={0: 0},
        cost_estimate=LONG,
        name="after",
    )(x, *deps)


def other_core(x):
    return lax.ppermute(x, "rows", [(i, i ^ 1) for i in range(4)])


def row_terms(mine, theirs, *deps):
    near = mine + other_core(theirs)
    if deps:
        near = after(near, *deps)
    return near, lax.ppermute(near, "rows", [(i, i ^ 2) for i in range(4)])


def body(matrix):
    index = lax.axis_index("pair")
    last = lax.axis_size("pair") - 1
    first_one, last_one = index == 0, index == last
    core = lax.axis_index("rows") % 2
    flags = jnp.stack([first_one, last_one, core]).astype(jnp.int32)

    near, far = row_terms(*gram_rows(flags, matrix, "gram_1"))
    (y1,) = factors(flags, near, far, "factors_1")
    y1 = (y1, other_core(y1))
    r1_3, l1_0 = rotate_rows(flags, y1, [(3, 0), (0, 1)], matrix, "rotate_1_ends")
    in_left = send_on(r1_3)
    in_right = send_back(l1_0)
    r1_0, l1_3, r1_1, l1_1, r1_2, l1_2 = rotate_rows(
        flags, y1, [(0, 0), (3, 1), (1, None), (2, None)], matrix, "rotate_1_inner"
    )
    in_left2 = send_on(r1_2)

    in_left = jnp.where(first_one, l1_0, in_left)
    in_right = jnp.where(last_one, r1_3, in_right)
    pairs2 = [(in_left, l1_1), (r1_0, l1_2), (r1_1, l1_3), (r1_2, in_right)]
    near, far = row_terms(*[gram_blocks(flags, pairs2, "gram_2")] * 2, in_left2)
    l1_1 = after(l1_1, near)
    pairs2[0] = (in_left, l1_1)
    in_right2 = send_back(l1_1)
    y2, to_left, to_right = factors(flags, near, far, "factors_2")
    edges2 = (send_on(to_right), send_back(to_left))
    r2_2, l2_1 = rotate_blocks(flags, (y2,), [(2, 0), (1, 1)], pairs2, "rotate_2_ends")
    in_left3 = send_on(r2_2)
    r2_0, l2_0, r2_3, l2_3, r2_1, l2_2 = rotate_blocks(
        flags, (y2,), [(0, None), (3, None), (1, 0), (2, 1)], pairs2, "rotate_2_inner", edges2
    )

    r2_left, l2_right = rotate_ends(
        flags, edges2, (in_left2, l1_0), (r1_3, in_right2), (l2_0, r2_3), "ends_2"
    )
    pairs3 = [(r2_left, l2_1), (r2_0, l2_2), (r2_1, l2_3), (r2_2, l2_right)]
    near, far = row_terms(*[gram_blocks(flags, pairs3, "gram_3")] * 2, in_left3)
    l2_1 = after(l2_1, near)
    pairs3[0] = (r2_left, l2_1)
    in_right3 = send_back(l2_1)
    y3, to_left, to_right = factors(flags, near, far, "factors_3")
    edges3 = (send_on(to_right), send_back(to_left))
    inner, *done = final_inner(flags, y3, pairs3)
    return final(flags, edges3, (in_left3, l2_0), (r2_3, in_right3), done, inner)


def solution(mesh):
    spec = P("rows", "pair")
    return jax.shard_map(body, mesh=mesh, in_specs=(spec,), out_specs=spec, check_vma=False)
```

```python
import functools

import jax
import jax.numpy as jnp
from jax import lax
from jax.experimental import pallas as pl
from jax.experimental.pallas import tpu as pltpu
from jax.sharding import PartitionSpec as P

B = 64
W = 128
PD = 4
NS_STEPS = 8
EPS = 1e-06
F32 = jnp.float32
BF16 = jnp.bfloat16

LONG = pl.CostEstimate(flops=10**10, bytes_accessed=4 * 10**8, transcendentals=0)

NN = (((1,), (0,)), ((), ()))
NT = (((1,), (1,)), ((), ()))
TN = (((0,), (0,)), ((), ()))


def params(mib=60):
    return pltpu.CompilerParams(vmem_limit_bytes=mib * 1024 * 1024)


def split(x):
    high = x.astype(BF16)
    return high, (x - high.astype(F32)).astype(BF16)


def dot(a, b, dims):
    return lax.dot_general(a, b, dims, preferred_element_type=F32)


def factor_stack(y):
    high, low = split(y)
    return jnp.concatenate(
        [jnp.concatenate([high, high], 1), jnp.concatenate([low, jnp.zeros_like(low)], 1)], 0
    )


def apply_rows(stack, values):
    high, low = split(values)
    both = dot(stack, jnp.concatenate([high, low], 0), NN)
    half = both.shape[0] // 2
    return both[:half] + both[half:]


def finish_gram(acc):
    cross = acc[:, W:]
    return acc[:, :W] + cross + cross.T


def store_gram(acc, mine, theirs):
    half = PD // 2
    core = lax.axis_index("rows") % 2
    for j in range(half):
        mine[j] = finish_gram(acc[core * half + j])
        theirs[j] = finish_gram(acc[(1 - core) * half + j])


def gram_rows_kernel(*refs):
    cols, (mine, theirs, acc) = refs[:PD], refs[PD:]
    step = pl.program_id(0)

    @pl.when(step == 0)
    def _():
        acc[...] = jnp.zeros_like(acc)

    for k in range(PD):
        high, low = split(cols[k][...])
        acc[k] += dot(high, jnp.concatenate([high, low], 1), TN)

    @pl.when(step == pl.num_programs(0) - 1)
    def _():
        store_gram(acc, mine, theirs)


def gram_blocks_kernel(*refs):
    blocks, (grams, acc) = refs[: 2 * PD], refs[2 * PD :]
    step = pl.program_id(0)

    @pl.when(step == 0)
    def _():
        acc[...] = jnp.zeros_like(acc)

    for k in range(PD):
        high, low = split(jnp.concatenate([blocks[2 * k][...], blocks[2 * k + 1][...]], 0))
        acc[k] += dot(high, jnp.concatenate([high, low], 0), NT)

    @pl.when(step == pl.num_programs(0) - 1)
    def _():
        for k in range(PD):
            grams[k] = finish_gram(acc[k])


SMEM_SPEC = pl.BlockSpec(memory_space=pltpu.SMEM)
ANY_SPEC = pl.BlockSpec(memory_space=pl.ANY)


def gram_call(kernel, operands, specs, steps, counts, name):
    return pl.pallas_call(
        kernel,
        grid=(steps,),
        in_specs=specs,
        out_specs=[pl.BlockSpec((n, W, W), lambda i: (0, 0, 0)) for n in counts],
        out_shape=[jax.ShapeDtypeStruct((n, W, W), F32) for n in counts],
        scratch_shapes=[pltpu.VMEM((PD, W, 2 * W), F32)],
        compiler_params=params(),
        cost_estimate=LONG,
        name=name,
    )(*operands)


def column_spec(k, chunk):
    return pl.BlockSpec((chunk, W), lambda i: (i, k))


def gram_rows(matrix, name, chunk=2048):
    specs = [column_spec(k, chunk) for k in range(PD)]
    steps, counts = matrix.shape[0] // chunk, (PD // 2, PD // 2)
    return gram_call(gram_rows_kernel, [matrix] * PD, specs, steps, counts, name)


def gram_blocks(pairs, name, chunk=2048):
    blocks = [x for pair in pairs for x in pair]
    specs = [pl.BlockSpec((B, chunk), lambda i: (0, i))] * len(blocks)
    steps = blocks[0].shape[1] // chunk
    return gram_call(gram_blocks_kernel, blocks, specs, steps, (PD,), name)[0]


def mm3(a, b, dims):
    ah, al = split(a)
    bh, bl = split(b)
    zero = jnp.zeros_like(bl)
    if dims == NT:
        right = jnp.concatenate([jnp.concatenate([bh, bh], 1), jnp.concatenate([bl, zero], 1)], 0)
    else:
        right = jnp.concatenate([jnp.concatenate([bh, bl], 1), jnp.concatenate([bh, zero], 1)], 0)
    out = dot(jnp.concatenate([ah, al], 1), right, dims)
    return out[:, :W] + out[:, W:]


def factors_kernel(flags, a_ref, b_ref, y_ref, *edges):
    row = lax.broadcasted_iota(jnp.int32, (W, W), 0)
    col = lax.broadcasted_iota(jnp.int32, (W, W), 1)
    eye = row == col
    n = y_ref.shape[0]
    ys = []
    for k in range(n):
        g = a_ref[k] + b_ref[k]
        diag = jnp.where(eye, g, 0.0)
        norm_col = jnp.sqrt(jnp.sum(diag, axis=1, keepdims=True) + EPS)
        norm_row = jnp.sqrt(jnp.sum(diag, axis=0, keepdims=True) + EPS)
        corr = g / (norm_col * norm_row)
        skew = jnp.where(row < col, -0.5 * corr, jnp.where(row > col, 0.5 * corr, 0.0))
        total = jnp.sum(jnp.sum(skew * skew, axis=1, keepdims=True), axis=0, keepdims=True)
        ys.append((jnp.where(eye, 1.0, 0.0) - skew) / jnp.sqrt(1.0 + total))

    def step(_, ys):
        inner = [mm3(y, y, NT) for y in ys]
        return tuple(1.5 * y - 0.5 * mm3(a, y, NN) for a, y in zip(inner, ys))

    ys = list(lax.fori_loop(0, NS_STEPS, step, tuple(ys)))
    swap = flags[0] != 0
    if n < PD:
        swap = jnp.logical_and(swap, flags[2] == 0)
    ys[0] = jnp.where(swap, jnp.concatenate([ys[0][B:], ys[0][:B]], 0), ys[0])
    for k in range(n):
        y_ref[k] = ys[k]
    if edges:
        edges[0][...] = ys[0][B:]
        edges[1][...] = ys[n - 1][:B]


def factors(flags, a, b, name):
    vmem = pl.BlockSpec(memory_space=pltpu.VMEM)
    edges = 2 if a.shape[0] == PD else 0
    return pl.pallas_call(
        factors_kernel,
        in_specs=[SMEM_SPEC, vmem, vmem],
        out_specs=[vmem] * (1 + edges),
        out_shape=[jax.ShapeDtypeStruct(a.shape, F32)] + [jax.ShapeDtypeStruct((B, W), F32)] * edges,
        compiler_params=params(),
        cost_estimate=LONG,
        name=name,
    )(flags, a, b)


def factor_of(flags, ys, k, half=None):
    if len(ys) == 1:
        y = ys[0][k]
    else:
        core, slot = divmod(k, PD // 2)
        y = jnp.where(flags[2] == core, ys[0][slot], ys[1][slot])
    return y if half is None else y[half * B : (half + 1) * B]


def rotate_kernel(parts, by_rows, sources, deps, flags, *refs):
    per = 1 if by_rows else 2
    ys, refs = refs[:sources], refs[sources:]
    ins, outs = refs[: per * len(parts)], list(refs[per * len(parts) + deps :])
    for at, (k, half) in enumerate(parts):
        y = factor_of(flags, ys, k, half)
        count = y.shape[0]
        if by_rows:
            high, low = split(ins[at][...])
            both = dot(factor_stack(y), jnp.concatenate([high, low], 1), NT)
            new = both[:count] + both[count:]
        else:
            new = apply_rows(
                factor_stack(y), jnp.concatenate([ins[2 * at][...], ins[2 * at + 1][...]], 0)
            )
        for start in range(0, count, B):
            outs.pop(0)[...] = new[start : start + B]


def rotate_call(flags, ys, parts, by_rows, operands, specs, cols, chunk, name, deps=()):
    count = sum(2 if half is None else 1 for _, half in parts)
    whole = pl.BlockSpec(ys[0].shape, lambda i: (0, 0, 0))
    return pl.pallas_call(
        functools.partial(rotate_kernel, parts, by_rows, len(ys), len(deps)),
        grid=(cols // chunk,),
        in_specs=[SMEM_SPEC] + [whole] * len(ys) + specs + [ANY_SPEC] * len(deps),
        out_specs=[pl.BlockSpec((B, chunk), lambda i: (0, i))] * count,
        out_shape=[jax.ShapeDtypeStruct((B, cols), F32)] * count,
        compiler_params=params(),
        cost_estimate=LONG,
        name=name,
    )(flags, *ys, *operands, *deps)


def rotate_rows(flags, ys, parts, matrix, name, chunk=2048):
    specs = [column_spec(k, chunk) for k, _ in parts]
    operands = [matrix] * len(parts)
    return rotate_call(flags, ys, parts, True, operands, specs, matrix.shape[0], chunk, name)


def rotate_blocks(flags, ys, parts, pairs, name, deps=(), chunk=2048):
    blocks = [x for k, _ in parts for x in pairs[k]]
    specs = [pl.BlockSpec((B, chunk), lambda i: (0, i))] * len(blocks)
    cols = blocks[0].shape[1]
    return rotate_call(flags, ys, parts, False, blocks, specs, cols, chunk, name, deps)


def round_2_rest_kernel(flags, y_ref, y_left, y_right, *refs):
    step = pl.program_id(0)
    left, p0, p1, p2, p3, right = [
        jnp.concatenate([refs[2 * k][...], refs[2 * k + 1][...]], 0) for k in range(PD + 2)
    ]
    r2, l1 = refs[2 * PD + 4][...], refs[2 * PD + 5][...]
    r_left, r_0, l_0, r_1, l_2, r_3, l_3, l_right, grams, acc = refs[2 * PD + 6 :]

    def rotated(y, values):
        return apply_rows(factor_stack(y), values)

    new0, new3 = rotated(y_ref[0], p0), rotated(y_ref[3], p3)
    r0, l0, r3, l3 = new0[:B], new0[B:], new3[:B], new3[B:]
    r1, l2 = rotated(y_ref[1][:B], p1), rotated(y_ref[2][B:], p2)
    rl = jnp.where(flags[0] != 0, l0, rotated(y_left[...], left))
    lr = jnp.where(flags[1] != 0, r3, rotated(y_right[...], right))
    for ref, value in zip(
        (r_left, r_0, l_0, r_1, l_2, r_3, l_3, l_right), (rl, r0, l0, r1, l2, r3, l3, lr)
    ):
        ref[...] = value

    @pl.when(step == 0)
    def _():
        acc[...] = jnp.zeros_like(acc)

    for k, (top, bottom) in enumerate([(rl, l1), (r0, l2), (r1, l3), (r2, lr)]):
        high, low = split(jnp.concatenate([top, bottom], 0))
        acc[k] += dot(high, jnp.concatenate([high, low], 0), NT)

    @pl.when(step == pl.num_programs(0) - 1)
    def _():
        for k in range(PD):
            grams[k] = finish_gram(acc[k])


def round_2_rest(flags, y, edges, pairs, left_pair, right_pair, done, chunk=1024):
    blocks = [*left_pair, *[x for pair in pairs for x in pair], *right_pair, *done]
    cols = done[0].shape[1]
    spec = pl.BlockSpec((B, chunk), lambda i: (0, i))
    half = pl.BlockSpec((B, W), lambda i: (0, 0))
    whole = pl.BlockSpec((PD, W, W), lambda i: (0, 0, 0))
    return pl.pallas_call(
        round_2_rest_kernel,
        grid=(cols // chunk,),
        in_specs=[SMEM_SPEC, whole, half, half] + [spec] * len(blocks),
        out_specs=[spec] * 8 + [whole],
        out_shape=[jax.ShapeDtypeStruct((B, cols), F32)] * 8
        + [jax.ShapeDtypeStruct((PD, W, W), F32)],
        scratch_shapes=[pltpu.VMEM((PD, W, 2 * W), F32)],
        compiler_params=params(),
        cost_estimate=LONG,
        name="round_2_rest",
    )(flags, y, *edges, *blocks)


def final_inner_kernel(flags, y_ref, *refs):
    ins = refs[: 2 * PD]
    out, l_1, r_2, l_0, r_3 = refs[2 * PD :]

    def rotated(k, half):
        values = jnp.concatenate([ins[2 * k][...], ins[2 * k + 1][...]], 0)
        return apply_rows(factor_stack(factor_of(flags, (y_ref,), k, half)), values)

    own1, own2 = rotated(1, None), rotated(2, None)
    l_1[...] = own1[B:]
    r_2[...] = own2[:B]
    out[:, :W] = jnp.concatenate([rotated(0, 0), own2[B:]], 0).T
    out[:, W:] = jnp.concatenate([own1[:B], rotated(3, 1)], 0).T

    @pl.when(flags[0] != 0)
    def _():
        l_0[...] = rotated(0, 1)

    @pl.when(flags[1] != 0)
    def _():
        r_3[...] = rotated(3, 0)


def edge_specs(chunk):
    return [
        pl.BlockSpec((B, chunk), lambda i, flags: (0, i * flags[0])),
        pl.BlockSpec((B, chunk), lambda i, flags: (0, i * flags[1])),
    ]


def final_inner(flags, y, pairs, chunk=2048):
    blocks = [x for pair in pairs for x in pair]
    cols = blocks[0].shape[1]
    spec = pl.BlockSpec((B, chunk), lambda i, flags: (0, i))
    block = jax.ShapeDtypeStruct((B, cols), F32)
    whole = pl.BlockSpec((PD, W, W), lambda i, flags: (0, 0, 0))
    return pl.pallas_call(
        final_inner_kernel,
        grid_spec=pltpu.PrefetchScalarGridSpec(
            num_scalar_prefetch=1,
            grid=(cols // chunk,),
            in_specs=[whole] + [spec] * len(blocks),
            out_specs=[pl.BlockSpec((chunk, 2 * W), lambda i, flags: (i, 0)), spec, spec]
            + edge_specs(chunk),
        ),
        out_shape=[jax.ShapeDtypeStruct((cols, 2 * W), F32)] + [block] * 4,
        compiler_params=params(),
        cost_estimate=LONG,
        name="final_inner",
    )(flags, y, *blocks)


def final_kernel(flags, y_left, y_right, lt, lb, rt, rb, l_1, r_2, l_0, r_3, inner, out):
    left = apply_rows(factor_stack(y_left[...]), jnp.concatenate([lt[...], lb[...]], 0))
    right = apply_rows(factor_stack(y_right[...]), jnp.concatenate([rt[...], rb[...]], 0))
    left = jnp.where(flags[0] != 0, l_0[...], left)
    right = jnp.where(flags[1] != 0, r_3[...], right)
    out[:, :W] = jnp.concatenate([left, l_1[...]], 0).T
    out[:, W : 3 * W] = inner[...]
    out[:, 3 * W :] = jnp.concatenate([r_2[...], right], 0).T


def final(flags, edges, left_pair, right_pair, done, inner, chunk=2048):
    cols = inner.shape[0]
    spec = pl.BlockSpec((B, chunk), lambda i, flags: (0, i))
    half = pl.BlockSpec((B, W), lambda i, flags: (0, 0))
    return pl.pallas_call(
        final_kernel,
        grid_spec=pltpu.PrefetchScalarGridSpec(
            num_scalar_prefetch=1,
            grid=(cols // chunk,),
            in_specs=[half, half]
            + [spec] * 6
            + edge_specs(chunk)
            + [pl.BlockSpec((chunk, 2 * W), lambda i, flags: (i, 0))],
            out_specs=pl.BlockSpec((chunk, PD * W), lambda i, flags: (i, 0)),
        ),
        out_shape=jax.ShapeDtypeStruct((cols, PD * W), F32),
        compiler_params=params(),
        cost_estimate=LONG,
        name="final",
    )(flags, *edges, *left_pair, *right_pair, *done, inner)


def send_on(x):
    peers = lax.axis_size("pair")
    return lax.ppermute(x, "pair", [(i, i + 1) for i in range(peers - 1)])


def send_back(x):
    peers = lax.axis_size("pair")
    return lax.ppermute(x, "pair", [(i + 1, i) for i in range(peers - 1)])


def after(x, *deps):
    return pl.pallas_call(
        lambda *refs: None,
        in_specs=[pl.BlockSpec(memory_space=pl.ANY)] * (1 + len(deps)),
        out_specs=pl.BlockSpec(memory_space=pl.ANY),
        out_shape=jax.ShapeDtypeStruct(x.shape, x.dtype),
        input_output_aliases={0: 0},
        cost_estimate=LONG,
        name="after",
    )(x, *deps)


def other_core(x):
    return lax.ppermute(x, "rows", [(i, i ^ 1) for i in range(4)])


def row_terms(mine, theirs):
    near = mine + other_core(theirs)
    return near, lax.ppermute(near, "rows", [(i, i ^ 2) for i in range(4)])


def body(matrix):
    index = lax.axis_index("pair")
    last = lax.axis_size("pair") - 1
    first_one, last_one = index == 0, index == last
    core = lax.axis_index("rows") % 2
    flags = jnp.stack([first_one, last_one, core]).astype(jnp.int32)

    near, far = row_terms(*gram_rows(matrix, "gram_1"))
    (y1,) = factors(flags, near, far, "factors_1")
    y1 = (y1, other_core(y1))
    r1_3, l1_0 = rotate_rows(flags, y1, [(3, 0), (0, 1)], matrix, "rotate_1_ends")
    in_left = send_on(r1_3)
    in_right = send_back(l1_0)
    r1_0, l1_3, r1_1, l1_1, r1_2, l1_2 = rotate_rows(
        flags, y1, [(0, 0), (3, 1), (1, None), (2, None)], matrix, "rotate_1_inner"
    )
    in_left2 = send_on(r1_2)

    in_left = jnp.where(first_one, l1_0, in_left)
    in_right = jnp.where(last_one, r1_3, in_right)
    pairs2 = [(in_left, l1_1), (r1_0, l1_2), (r1_1, l1_3), (r1_2, in_right)]
    near, far = row_terms(*[gram_blocks(pairs2, "gram_2")] * 2)
    l1_1 = after(l1_1, near, in_left2)
    pairs2[0] = (in_left, l1_1)
    in_right2 = send_back(l1_1)
    y2, to_left, to_right = factors(flags, near, far, "factors_2")
    edges2 = (send_on(to_right), send_back(to_left))
    r2_2, l2_1 = rotate_blocks(flags, (y2,), [(2, 0), (1, 1)], pairs2, "rotate_2_ends")
    in_left3 = send_on(r2_2)
    r2_left, r2_0, l2_0, r2_1, l2_2, r2_3, l2_3, l2_right, gram = round_2_rest(
        flags, y2, edges2, pairs2, (in_left2, l1_0), (r1_3, in_right2), (r2_2, l2_1)
    )

    pairs3 = [(r2_left, l2_1), (r2_0, l2_2), (r2_1, l2_3), (r2_2, l2_right)]
    near, far = row_terms(gram, gram)
    l2_1 = after(l2_1, near, in_left3)
    pairs3[0] = (r2_left, l2_1)
    in_right3 = send_back(l2_1)
    y3, to_left, to_right = factors(flags, near, far, "factors_3")
    edges3 = (send_on(to_right), send_back(to_left))
    inner, *done = final_inner(flags, y3, pairs3)
    return final(flags, edges3, (in_left3, l2_0), (r2_3, in_right3), done, inner)


def solution(mesh):
    spec = P("rows", "pair")
    return jax.shard_map(body, mesh=mesh, in_specs=(spec,), out_specs=spec, check_vma=False)
```

```python
import functools

import jax
import jax.numpy as jnp
from jax import lax
from jax.experimental import pallas as pl
from jax.experimental.pallas import tpu as pltpu
from jax.sharding import PartitionSpec as P

B = 64
W = 128
PD = 4
NS_STEPS = 8
EPS = 1e-06
F32 = jnp.float32
BF16 = jnp.bfloat16

LONG = pl.CostEstimate(flops=10**10, bytes_accessed=4 * 10**8, transcendentals=0)

NN = (((1,), (0,)), ((), ()))
NT = (((1,), (1,)), ((), ()))
TN = (((0,), (0,)), ((), ()))


def params(mib=60):
    return pltpu.CompilerParams(vmem_limit_bytes=mib * 1024 * 1024)


def split(x):
    high = x.astype(BF16)
    return high, (x - high.astype(F32)).astype(BF16)


def dot(a, b, dims):
    return lax.dot_general(a, b, dims, preferred_element_type=F32)


def factor_stack(y):
    high, low = split(y)
    return jnp.concatenate(
        [jnp.concatenate([high, high], 1), jnp.concatenate([low, jnp.zeros_like(low)], 1)], 0
    )


def apply_rows(stack, values):
    high, low = split(values)
    both = dot(stack, jnp.concatenate([high, low], 0), NN)
    half = both.shape[0] // 2
    return both[:half] + both[half:]


def finish_gram(acc):
    cross = acc[:, W:]
    return acc[:, :W] + cross + cross.T


def store_gram(acc, mine, theirs):
    half = PD // 2
    core = lax.axis_index("rows") % 2
    for j in range(half):
        mine[j] = finish_gram(acc[core * half + j])
        theirs[j] = finish_gram(acc[(1 - core) * half + j])


def gram_rows_kernel(*refs):
    cols, (mine, theirs, acc) = refs[:PD], refs[PD:]
    step = pl.program_id(0)

    @pl.when(step == 0)
    def _():
        acc[...] = jnp.zeros_like(acc)

    for k in range(PD):
        high, low = split(cols[k][...])
        acc[k] += dot(high, jnp.concatenate([high, low], 1), TN)

    @pl.when(step == pl.num_programs(0) - 1)
    def _():
        store_gram(acc, mine, theirs)


def gram_blocks_kernel(*refs):
    blocks, (grams, acc) = refs[: 2 * PD], refs[2 * PD :]
    step = pl.program_id(0)

    @pl.when(step == 0)
    def _():
        acc[...] = jnp.zeros_like(acc)

    for k in range(PD):
        high, low = split(jnp.concatenate([blocks[2 * k][...], blocks[2 * k + 1][...]], 0))
        acc[k] += dot(high, jnp.concatenate([high, low], 0), NT)

    @pl.when(step == pl.num_programs(0) - 1)
    def _():
        for k in range(PD):
            grams[k] = finish_gram(acc[k])


SMEM_SPEC = pl.BlockSpec(memory_space=pltpu.SMEM)
ANY_SPEC = pl.BlockSpec(memory_space=pl.ANY)


def gram_call(kernel, operands, specs, steps, counts, name):
    return pl.pallas_call(
        kernel,
        grid=(steps,),
        in_specs=specs,
        out_specs=[pl.BlockSpec((n, W, W), lambda i: (0, 0, 0)) for n in counts],
        out_shape=[jax.ShapeDtypeStruct((n, W, W), F32) for n in counts],
        scratch_shapes=[pltpu.VMEM((PD, W, 2 * W), F32)],
        compiler_params=params(56),
        cost_estimate=LONG,
        name=name,
    )(*operands)


def column_spec(k, chunk):
    return pl.BlockSpec((chunk, W), lambda i: (i, k))


def gram_rows(matrix, name, chunk=2048):
    specs = [column_spec(k, chunk) for k in range(PD)]
    steps, counts = matrix.shape[0] // chunk, (PD // 2, PD // 2)
    return gram_call(gram_rows_kernel, [matrix] * PD, specs, steps, counts, name)


def gram_blocks(pairs, name, chunk=2048):
    blocks = [x for pair in pairs for x in pair]
    specs = [pl.BlockSpec((B, chunk), lambda i: (0, i))] * len(blocks)
    steps = blocks[0].shape[1] // chunk
    return gram_call(gram_blocks_kernel, blocks, specs, steps, (PD,), name)[0]


def mm3(a, b, dims):
    ah, al = split(a)
    bh, bl = split(b)
    zero = jnp.zeros_like(bl)
    if dims == NT:
        right = jnp.concatenate([jnp.concatenate([bh, bh], 1), jnp.concatenate([bl, zero], 1)], 0)
    else:
        right = jnp.concatenate([jnp.concatenate([bh, bl], 1), jnp.concatenate([bh, zero], 1)], 0)
    out = dot(jnp.concatenate([ah, al], 1), right, dims)
    return out[:, :W] + out[:, W:]


def factors_kernel(flags, a_ref, b_ref, y_ref, *edges):
    row = lax.broadcasted_iota(jnp.int32, (W, W), 0)
    col = lax.broadcasted_iota(jnp.int32, (W, W), 1)
    eye = row == col
    n = y_ref.shape[0]
    ys = []
    for k in range(n):
        g = a_ref[k] + b_ref[k]
        diag = jnp.where(eye, g, 0.0)
        norm_col = jnp.sqrt(jnp.sum(diag, axis=1, keepdims=True) + EPS)
        norm_row = jnp.sqrt(jnp.sum(diag, axis=0, keepdims=True) + EPS)
        corr = g / (norm_col * norm_row)
        skew = jnp.where(row < col, -0.5 * corr, jnp.where(row > col, 0.5 * corr, 0.0))
        total = jnp.sum(jnp.sum(skew * skew, axis=1, keepdims=True), axis=0, keepdims=True)
        ys.append((jnp.where(eye, 1.0, 0.0) - skew) / jnp.sqrt(1.0 + total))

    def step(_, ys):
        inner = [mm3(y, y, NT) for y in ys]
        return tuple(1.5 * y - 0.5 * mm3(a, y, NN) for a, y in zip(inner, ys))

    ys = list(lax.fori_loop(0, NS_STEPS, step, tuple(ys)))
    swap = flags[0] != 0
    if n < PD:
        swap = jnp.logical_and(swap, flags[2] == 0)
    ys[0] = jnp.where(swap, jnp.concatenate([ys[0][B:], ys[0][:B]], 0), ys[0])
    for k in range(n):
        y_ref[k] = ys[k]
    if edges:
        edges[0][...] = ys[0][B:]
        edges[1][...] = ys[n - 1][:B]


def factors(flags, a, b, name):
    vmem = pl.BlockSpec(memory_space=pltpu.VMEM)
    edges = 2 if a.shape[0] == PD else 0
    return pl.pallas_call(
        factors_kernel,
        in_specs=[SMEM_SPEC, vmem, vmem],
        out_specs=[vmem] * (1 + edges),
        out_shape=[jax.ShapeDtypeStruct(a.shape, F32)] + [jax.ShapeDtypeStruct((B, W), F32)] * edges,
        compiler_params=params(40),
        cost_estimate=LONG,
        name=name,
    )(flags, a, b)


def factor_of(flags, ys, k, half=None):
    if len(ys) == 1:
        y = ys[0][k]
    else:
        core, slot = divmod(k, PD // 2)
        y = jnp.where(flags[2] == core, ys[0][slot], ys[1][slot])
    return y if half is None else y[half * B : (half + 1) * B]


def rotate_kernel(parts, by_rows, sources, deps, flags, *refs):
    per = 1 if by_rows else 2
    ys, refs = refs[:sources], refs[sources:]
    ins, outs = refs[: per * len(parts)], list(refs[per * len(parts) + deps :])
    for at, (k, half) in enumerate(parts):
        y = factor_of(flags, ys, k, half)
        count = y.shape[0]
        if by_rows:
            high, low = split(ins[at][...])
            both = dot(factor_stack(y), jnp.concatenate([high, low], 1), NT)
            new = both[:count] + both[count:]
        else:
            new = apply_rows(
                factor_stack(y), jnp.concatenate([ins[2 * at][...], ins[2 * at + 1][...]], 0)
            )
        for start in range(0, count, B):
            outs.pop(0)[...] = new[start : start + B]


def rotate_call(flags, ys, parts, by_rows, operands, specs, cols, chunk, name, deps=()):
    count = sum(2 if half is None else 1 for _, half in parts)
    whole = pl.BlockSpec(ys[0].shape, lambda i: (0, 0, 0))
    return pl.pallas_call(
        functools.partial(rotate_kernel, parts, by_rows, len(ys), len(deps)),
        grid=(cols // chunk,),
        in_specs=[SMEM_SPEC] + [whole] * len(ys) + specs + [ANY_SPEC] * len(deps),
        out_specs=[pl.BlockSpec((B, chunk), lambda i: (0, i))] * count,
        out_shape=[jax.ShapeDtypeStruct((B, cols), F32)] * count,
        compiler_params=params(56),
        cost_estimate=LONG,
        name=name,
    )(flags, *ys, *operands, *deps)


def rotate_rows(flags, ys, parts, matrix, name, chunk=2048):
    specs = [column_spec(k, chunk) for k, _ in parts]
    operands = [matrix] * len(parts)
    return rotate_call(flags, ys, parts, True, operands, specs, matrix.shape[0], chunk, name)


def rotate_blocks(flags, ys, parts, pairs, name, deps=(), chunk=2048):
    blocks = [x for k, _ in parts for x in pairs[k]]
    specs = [pl.BlockSpec((B, chunk), lambda i: (0, i))] * len(blocks)
    cols = blocks[0].shape[1]
    return rotate_call(flags, ys, parts, False, blocks, specs, cols, chunk, name, deps)


def round_2_rest_kernel(flags, y_ref, y_left, y_right, *refs):
    step = pl.program_id(0)
    left, p0, p1, p2, p3, right = [
        jnp.concatenate([refs[2 * k][...], refs[2 * k + 1][...]], 0) for k in range(PD + 2)
    ]
    r2, l1 = refs[2 * PD + 4][...], refs[2 * PD + 5][...]
    r_left, r_0, l_0, r_1, l_2, r_3, l_3, l_right, grams, acc = refs[2 * PD + 6 :]

    def rotated(y, values):
        return apply_rows(factor_stack(y), values)

    new0, new3 = rotated(y_ref[0], p0), rotated(y_ref[3], p3)
    r0, l0, r3, l3 = new0[:B], new0[B:], new3[:B], new3[B:]
    r1, l2 = rotated(y_ref[1][:B], p1), rotated(y_ref[2][B:], p2)
    rl = jnp.where(flags[0] != 0, l0, rotated(y_left[...], left))
    lr = jnp.where(flags[1] != 0, r3, rotated(y_right[...], right))
    for ref, value in zip(
        (r_left, r_0, l_0, r_1, l_2, r_3, l_3, l_right), (rl, r0, l0, r1, l2, r3, l3, lr)
    ):
        ref[...] = value

    @pl.when(step == 0)
    def _():
        acc[...] = jnp.zeros_like(acc)

    for k, (top, bottom) in enumerate([(rl, l1), (r0, l2), (r1, l3), (r2, lr)]):
        high, low = split(jnp.concatenate([top, bottom], 0))
        acc[k] += dot(high, jnp.concatenate([high, low], 0), NT)

    @pl.when(step == pl.num_programs(0) - 1)
    def _():
        for k in range(PD):
            grams[k] = finish_gram(acc[k])


def round_2_rest(flags, y, edges, pairs, left_pair, right_pair, done, chunk=1024):
    blocks = [*left_pair, *[x for pair in pairs for x in pair], *right_pair, *done]
    cols = done[0].shape[1]
    spec = pl.BlockSpec((B, chunk), lambda i: (0, i))
    half = pl.BlockSpec((B, W), lambda i: (0, 0))
    whole = pl.BlockSpec((PD, W, W), lambda i: (0, 0, 0))
    return pl.pallas_call(
        round_2_rest_kernel,
        grid=(cols // chunk,),
        in_specs=[SMEM_SPEC, whole, half, half] + [spec] * len(blocks),
        out_specs=[spec] * 8 + [whole],
        out_shape=[jax.ShapeDtypeStruct((B, cols), F32)] * 8
        + [jax.ShapeDtypeStruct((PD, W, W), F32)],
        scratch_shapes=[pltpu.VMEM((PD, W, 2 * W), F32)],
        compiler_params=params(),
        cost_estimate=LONG,
        name="round_2_rest",
    )(flags, y, *edges, *blocks)


def final_inner_kernel(flags, y_ref, *refs):
    ins = refs[: 2 * PD]
    out, l_1, r_2, l_0, r_3 = refs[2 * PD :]

    def rotated(k, half):
        values = jnp.concatenate([ins[2 * k][...], ins[2 * k + 1][...]], 0)
        return apply_rows(factor_stack(factor_of(flags, (y_ref,), k, half)), values)

    own1, own2 = rotated(1, None), rotated(2, None)
    l_1[...] = own1[B:]
    r_2[...] = own2[:B]
    out[:, :W] = jnp.concatenate([rotated(0, 0), own2[B:]], 0).T
    out[:, W:] = jnp.concatenate([own1[:B], rotated(3, 1)], 0).T

    @pl.when(flags[0] != 0)
    def _():
        l_0[...] = rotated(0, 1)

    @pl.when(flags[1] != 0)
    def _():
        r_3[...] = rotated(3, 0)


def edge_specs(chunk):
    return [
        pl.BlockSpec((B, chunk), lambda i, flags: (0, i * flags[0])),
        pl.BlockSpec((B, chunk), lambda i, flags: (0, i * flags[1])),
    ]


def final_inner(flags, y, pairs, chunk=2048):
    blocks = [x for pair in pairs for x in pair]
    cols = blocks[0].shape[1]
    spec = pl.BlockSpec((B, chunk), lambda i, flags: (0, i))
    block = jax.ShapeDtypeStruct((B, cols), F32)
    whole = pl.BlockSpec((PD, W, W), lambda i, flags: (0, 0, 0))
    return pl.pallas_call(
        final_inner_kernel,
        grid_spec=pltpu.PrefetchScalarGridSpec(
            num_scalar_prefetch=1,
            grid=(cols // chunk,),
            in_specs=[whole] + [spec] * len(blocks),
            out_specs=[pl.BlockSpec((chunk, 2 * W), lambda i, flags: (i, 0)), spec, spec]
            + edge_specs(chunk),
        ),
        out_shape=[jax.ShapeDtypeStruct((cols, 2 * W), F32)] + [block] * 4,
        compiler_params=params(),
        cost_estimate=LONG,
        name="final_inner",
    )(flags, y, *blocks)


def final_kernel(flags, y_left, y_right, lt, lb, rt, rb, l_1, r_2, l_0, r_3, inner, out):
    left = apply_rows(factor_stack(y_left[...]), jnp.concatenate([lt[...], lb[...]], 0))
    right = apply_rows(factor_stack(y_right[...]), jnp.concatenate([rt[...], rb[...]], 0))
    left = jnp.where(flags[0] != 0, l_0[...], left)
    right = jnp.where(flags[1] != 0, r_3[...], right)
    out[:, :W] = jnp.concatenate([left, l_1[...]], 0).T
    out[:, W : 3 * W] = inner[...]
    out[:, 3 * W :] = jnp.concatenate([r_2[...], right], 0).T


def final(flags, edges, left_pair, right_pair, done, inner, chunk=2048):
    cols = inner.shape[0]
    spec = pl.BlockSpec((B, chunk), lambda i, flags: (0, i))
    half = pl.BlockSpec((B, W), lambda i, flags: (0, 0))
    return pl.pallas_call(
        final_kernel,
        grid_spec=pltpu.PrefetchScalarGridSpec(
            num_scalar_prefetch=1,
            grid=(cols // chunk,),
            in_specs=[half, half]
            + [spec] * 6
            + edge_specs(chunk)
            + [pl.BlockSpec((chunk, 2 * W), lambda i, flags: (i, 0))],
            out_specs=pl.BlockSpec((chunk, PD * W), lambda i, flags: (i, 0)),
        ),
        out_shape=jax.ShapeDtypeStruct((cols, PD * W), F32),
        compiler_params=params(),
        cost_estimate=LONG,
        name="final",
    )(flags, *edges, *left_pair, *right_pair, *done, inner)


def send_on(x):
    peers = lax.axis_size("pair")
    return lax.ppermute(x, "pair", [(i, i + 1) for i in range(peers - 1)])


def send_back(x):
    peers = lax.axis_size("pair")
    return lax.ppermute(x, "pair", [(i + 1, i) for i in range(peers - 1)])


def after(x, *deps):
    return pl.pallas_call(
        lambda *refs: None,
        in_specs=[pl.BlockSpec(memory_space=pl.ANY)] * (1 + len(deps)),
        out_specs=pl.BlockSpec(memory_space=pl.ANY),
        out_shape=jax.ShapeDtypeStruct(x.shape, x.dtype),
        input_output_aliases={0: 0},
        cost_estimate=LONG,
        name="after",
    )(x, *deps)


def other_core(x):
    return lax.ppermute(x, "rows", [(i, i ^ 1) for i in range(4)])


def row_terms(mine, theirs):
    near = mine + other_core(theirs)
    return near, lax.ppermute(near, "rows", [(i, i ^ 2) for i in range(4)])


def body(matrix):
    index = lax.axis_index("pair")
    last = lax.axis_size("pair") - 1
    first_one, last_one = index == 0, index == last
    core = lax.axis_index("rows") % 2
    flags = jnp.stack([first_one, last_one, core]).astype(jnp.int32)

    near, far = row_terms(*gram_rows(matrix, "gram_1"))
    (y1,) = factors(flags, near, far, "factors_1")
    y1 = (y1, other_core(y1))
    r1_3, l1_0 = rotate_rows(flags, y1, [(3, 0), (0, 1)], matrix, "rotate_1_ends")
    in_left = send_on(r1_3)
    in_right = send_back(l1_0)
    r1_0, l1_3, r1_1, l1_1, r1_2, l1_2 = rotate_rows(
        flags, y1, [(0, 0), (3, 1), (1, None), (2, None)], matrix, "rotate_1_inner"
    )
    in_left2 = send_on(r1_2)

    in_left = jnp.where(first_one, l1_0, in_left)
    in_right = jnp.where(last_one, r1_3, in_right)
    pairs2 = [(in_left, l1_1), (r1_0, l1_2), (r1_1, l1_3), (r1_2, in_right)]
    near, far = row_terms(*[gram_blocks(pairs2, "gram_2")] * 2)
    l1_1 = after(l1_1, near, in_left2)
    pairs2[0] = (in_left, l1_1)
    in_right2 = send_back(l1_1)
    y2, to_left, to_right = factors(flags, near, far, "factors_2")
    edges2 = (send_on(to_right), send_back(to_left))
    r2_2, l2_1 = rotate_blocks(flags, (y2,), [(2, 0), (1, 1)], pairs2, "rotate_2_ends")
    in_left3 = send_on(r2_2)
    r2_left, r2_0, l2_0, r2_1, l2_2, r2_3, l2_3, l2_right, gram = round_2_rest(
        flags, y2, edges2, pairs2, (in_left2, l1_0), (r1_3, in_right2), (r2_2, l2_1)
    )

    pairs3 = [(r2_left, l2_1), (r2_0, l2_2), (r2_1, l2_3), (r2_2, l2_right)]
    near, far = row_terms(gram, gram)
    l2_1 = after(l2_1, near, in_left3)
    pairs3[0] = (r2_left, l2_1)
    in_right3 = send_back(l2_1)
    y3, to_left, to_right = factors(flags, near, far, "factors_3")
    edges3 = (send_on(to_right), send_back(to_left))
    inner, *done = final_inner(flags, y3, pairs3)
    return final(flags, edges3, (in_left3, l2_0), (r2_3, in_right3), done, inner)


def solution(mesh):
    spec = P("rows", "pair")
    return jax.shard_map(body, mesh=mesh, in_specs=(spec,), out_specs=spec, check_vma=False)
```

```python
import functools

import jax
import jax.numpy as jnp
from jax import lax
from jax.experimental import pallas as pl
from jax.experimental.pallas import tpu as pltpu
from jax.sharding import PartitionSpec as P

B = 64
W = 128
PD = 4
NS_STEPS = 8
EPS = 1e-06
F32 = jnp.float32
BF16 = jnp.bfloat16

LONG = pl.CostEstimate(flops=10**10, bytes_accessed=4 * 10**8, transcendentals=0)

NN = (((1,), (0,)), ((), ()))
NT = (((1,), (1,)), ((), ()))
TN = (((0,), (0,)), ((), ()))


def params(mib=60):
    return pltpu.CompilerParams(vmem_limit_bytes=mib * 1024 * 1024)


def split(x):
    high = x.astype(BF16)
    return high, (x - high.astype(F32)).astype(BF16)


def dot(a, b, dims):
    return lax.dot_general(a, b, dims, preferred_element_type=F32)


def factor_stack(y):
    high, low = split(y)
    return jnp.concatenate(
        [jnp.concatenate([high, high], 1), jnp.concatenate([low, jnp.zeros_like(low)], 1)], 0
    )


def apply_rows(stack, values):
    high, low = split(values)
    both = dot(stack, jnp.concatenate([high, low], 0), NN)
    half = both.shape[0] // 2
    return both[:half] + both[half:]


def finish_gram(acc):
    cross = acc[:, W:]
    return acc[:, :W] + cross + cross.T


def store_gram(acc, mine, theirs):
    half = PD // 2
    core = lax.axis_index("rows") % 2
    for j in range(half):
        mine[j] = finish_gram(acc[core * half + j])
        theirs[j] = finish_gram(acc[(1 - core) * half + j])


def gram_rows_kernel(*refs):
    cols, (mine, theirs, acc) = refs[:PD], refs[PD:]
    step = pl.program_id(0)

    @pl.when(step == 0)
    def _():
        acc[...] = jnp.zeros_like(acc)

    for k in range(PD):
        high, low = split(cols[k][...])
        acc[k] += dot(high, jnp.concatenate([high, low], 1), TN)

    @pl.when(step == pl.num_programs(0) - 1)
    def _():
        store_gram(acc, mine, theirs)


def gram_blocks_kernel(*refs):
    blocks, (grams, acc) = refs[: 2 * PD], refs[2 * PD :]
    step = pl.program_id(0)

    @pl.when(step == 0)
    def _():
        acc[...] = jnp.zeros_like(acc)

    for k in range(PD):
        high, low = split(jnp.concatenate([blocks[2 * k][...], blocks[2 * k + 1][...]], 0))
        acc[k] += dot(high, jnp.concatenate([high, low], 0), NT)

    @pl.when(step == pl.num_programs(0) - 1)
    def _():
        for k in range(PD):
            grams[k] = finish_gram(acc[k])


SMEM_SPEC = pl.BlockSpec(memory_space=pltpu.SMEM)
ANY_SPEC = pl.BlockSpec(memory_space=pl.ANY)


def gram_call(kernel, operands, specs, steps, counts, name):
    return pl.pallas_call(
        kernel,
        grid=(steps,),
        in_specs=specs,
        out_specs=[pl.BlockSpec((n, W, W), lambda i: (0, 0, 0)) for n in counts],
        out_shape=[jax.ShapeDtypeStruct((n, W, W), F32) for n in counts],
        scratch_shapes=[pltpu.VMEM((PD, W, 2 * W), F32)],
        compiler_params=params(52),
        cost_estimate=LONG,
        name=name,
    )(*operands)


def column_spec(k, chunk):
    return pl.BlockSpec((chunk, W), lambda i: (i, k))


def gram_rows(matrix, name, chunk=2048):
    specs = [column_spec(k, chunk) for k in range(PD)]
    steps, counts = matrix.shape[0] // chunk, (PD // 2, PD // 2)
    return gram_call(gram_rows_kernel, [matrix] * PD, specs, steps, counts, name)


def gram_blocks(pairs, name, chunk=2048):
    blocks = [x for pair in pairs for x in pair]
    specs = [pl.BlockSpec((B, chunk), lambda i: (0, i))] * len(blocks)
    steps = blocks[0].shape[1] // chunk
    return gram_call(gram_blocks_kernel, blocks, specs, steps, (PD,), name)[0]


def mm3(a, b, dims):
    ah, al = split(a)
    bh, bl = split(b)
    zero = jnp.zeros_like(bl)
    if dims == NT:
        right = jnp.concatenate([jnp.concatenate([bh, bh], 1), jnp.concatenate([bl, zero], 1)], 0)
    else:
        right = jnp.concatenate([jnp.concatenate([bh, bl], 1), jnp.concatenate([bh, zero], 1)], 0)
    out = dot(jnp.concatenate([ah, al], 1), right, dims)
    return out[:, :W] + out[:, W:]


def factors_kernel(flags, a_ref, b_ref, y_ref, *edges):
    row = lax.broadcasted_iota(jnp.int32, (W, W), 0)
    col = lax.broadcasted_iota(jnp.int32, (W, W), 1)
    eye = row == col
    n = y_ref.shape[0]
    ys = []
    for k in range(n):
        g = a_ref[k] + b_ref[k]
        diag = jnp.where(eye, g, 0.0)
        norm_col = jnp.sqrt(jnp.sum(diag, axis=1, keepdims=True) + EPS)
        norm_row = jnp.sqrt(jnp.sum(diag, axis=0, keepdims=True) + EPS)
        corr = g / (norm_col * norm_row)
        skew = jnp.where(row < col, -0.5 * corr, jnp.where(row > col, 0.5 * corr, 0.0))
        total = jnp.sum(jnp.sum(skew * skew, axis=1, keepdims=True), axis=0, keepdims=True)
        ys.append((jnp.where(eye, 1.0, 0.0) - skew) / jnp.sqrt(1.0 + total))

    def step(_, ys):
        inner = [mm3(y, y, NT) for y in ys]
        return tuple(1.5 * y - 0.5 * mm3(a, y, NN) for a, y in zip(inner, ys))

    ys = list(lax.fori_loop(0, NS_STEPS, step, tuple(ys)))
    swap = flags[0] != 0
    if n < PD:
        swap = jnp.logical_and(swap, flags[2] == 0)
    ys[0] = jnp.where(swap, jnp.concatenate([ys[0][B:], ys[0][:B]], 0), ys[0])
    for k in range(n):
        y_ref[k] = ys[k]
    if edges:
        edges[0][...] = ys[0][B:]
        edges[1][...] = ys[n - 1][:B]


def factors(flags, a, b, name):
    vmem = pl.BlockSpec(memory_space=pltpu.VMEM)
    edges = 2 if a.shape[0] == PD else 0
    return pl.pallas_call(
        factors_kernel,
        in_specs=[SMEM_SPEC, vmem, vmem],
        out_specs=[vmem] * (1 + edges),
        out_shape=[jax.ShapeDtypeStruct(a.shape, F32)] + [jax.ShapeDtypeStruct((B, W), F32)] * edges,
        compiler_params=params(40),
        cost_estimate=LONG,
        name=name,
    )(flags, a, b)


def factor_of(flags, ys, k, half=None):
    if len(ys) == 1:
        y = ys[0][k]
    else:
        core, slot = divmod(k, PD // 2)
        y = jnp.where(flags[2] == core, ys[0][slot], ys[1][slot])
    return y if half is None else y[half * B : (half + 1) * B]


def rotate_kernel(parts, by_rows, sources, deps, flags, *refs):
    per = 1 if by_rows else 2
    ys, refs = refs[:sources], refs[sources:]
    ins, outs = refs[: per * len(parts)], list(refs[per * len(parts) + deps :])
    for at, (k, half) in enumerate(parts):
        y = factor_of(flags, ys, k, half)
        count = y.shape[0]
        if by_rows:
            high, low = split(ins[at][...])
            both = dot(factor_stack(y), jnp.concatenate([high, low], 1), NT)
            new = both[:count] + both[count:]
        else:
            new = apply_rows(
                factor_stack(y), jnp.concatenate([ins[2 * at][...], ins[2 * at + 1][...]], 0)
            )
        for start in range(0, count, B):
            outs.pop(0)[...] = new[start : start + B]


def rotate_call(flags, ys, parts, by_rows, operands, specs, cols, chunk, name, deps=()):
    count = sum(2 if half is None else 1 for _, half in parts)
    whole = pl.BlockSpec(ys[0].shape, lambda i: (0, 0, 0))
    return pl.pallas_call(
        functools.partial(rotate_kernel, parts, by_rows, len(ys), len(deps)),
        grid=(cols // chunk,),
        in_specs=[SMEM_SPEC] + [whole] * len(ys) + specs + [ANY_SPEC] * len(deps),
        out_specs=[pl.BlockSpec((B, chunk), lambda i: (0, i))] * count,
        out_shape=[jax.ShapeDtypeStruct((B, cols), F32)] * count,
        compiler_params=params(56),
        cost_estimate=LONG,
        name=name,
    )(flags, *ys, *operands, *deps)


def rotate_rows(flags, ys, parts, matrix, name, chunk=2048):
    specs = [column_spec(k, chunk) for k, _ in parts]
    operands = [matrix] * len(parts)
    return rotate_call(flags, ys, parts, True, operands, specs, matrix.shape[0], chunk, name)


def rotate_blocks(flags, ys, parts, pairs, name, deps=(), chunk=2048):
    blocks = [x for k, _ in parts for x in pairs[k]]
    specs = [pl.BlockSpec((B, chunk), lambda i: (0, i))] * len(blocks)
    cols = blocks[0].shape[1]
    return rotate_call(flags, ys, parts, False, blocks, specs, cols, chunk, name, deps)


def round_2_rest_kernel(flags, y_ref, y_left, y_right, *refs):
    step = pl.program_id(0)
    left, p0, p1, p2, p3, right = [
        jnp.concatenate([refs[2 * k][...], refs[2 * k + 1][...]], 0) for k in range(PD + 2)
    ]
    r2, l1 = refs[2 * PD + 4][...], refs[2 * PD + 5][...]
    r_left, r_0, l_0, r_1, l_2, r_3, l_3, l_right, grams, acc = refs[2 * PD + 6 :]

    def rotated(y, values):
        return apply_rows(factor_stack(y), values)

    new0, new3 = rotated(y_ref[0], p0), rotated(y_ref[3], p3)
    r0, l0, r3, l3 = new0[:B], new0[B:], new3[:B], new3[B:]
    r1, l2 = rotated(y_ref[1][:B], p1), rotated(y_ref[2][B:], p2)
    rl = jnp.where(flags[0] != 0, l0, rotated(y_left[...], left))
    lr = jnp.where(flags[1] != 0, r3, rotated(y_right[...], right))
    for ref, value in zip(
        (r_left, r_0, l_0, r_1, l_2, r_3, l_3, l_right), (rl, r0, l0, r1, l2, r3, l3, lr)
    ):
        ref[...] = value

    @pl.when(step == 0)
    def _():
        acc[...] = jnp.zeros_like(acc)

    for k, (top, bottom) in enumerate([(rl, l1), (r0, l2), (r1, l3), (r2, lr)]):
        high, low = split(jnp.concatenate([top, bottom], 0))
        acc[k] += dot(high, jnp.concatenate([high, low], 0), NT)

    @pl.when(step == pl.num_programs(0) - 1)
    def _():
        for k in range(PD):
            grams[k] = finish_gram(acc[k])


def round_2_rest(flags, y, edges, pairs, left_pair, right_pair, done, chunk=1024):
    blocks = [*left_pair, *[x for pair in pairs for x in pair], *right_pair, *done]
    cols = done[0].shape[1]
    spec = pl.BlockSpec((B, chunk), lambda i: (0, i))
    half = pl.BlockSpec((B, W), lambda i: (0, 0))
    whole = pl.BlockSpec((PD, W, W), lambda i: (0, 0, 0))
    return pl.pallas_call(
        round_2_rest_kernel,
        grid=(cols // chunk,),
        in_specs=[SMEM_SPEC, whole, half, half] + [spec] * len(blocks),
        out_specs=[spec] * 8 + [whole],
        out_shape=[jax.ShapeDtypeStruct((B, cols), F32)] * 8
        + [jax.ShapeDtypeStruct((PD, W, W), F32)],
        scratch_shapes=[pltpu.VMEM((PD, W, 2 * W), F32)],
        compiler_params=params(),
        cost_estimate=LONG,
        name="round_2_rest",
    )(flags, y, *edges, *blocks)


def final_inner_kernel(flags, y_ref, *refs):
    ins = refs[: 2 * PD]
    out, l_1, r_2, l_0, r_3 = refs[2 * PD :]

    def rotated(k, half):
        values = jnp.concatenate([ins[2 * k][...], ins[2 * k + 1][...]], 0)
        return apply_rows(factor_stack(factor_of(flags, (y_ref,), k, half)), values)

    own1, own2 = rotated(1, None), rotated(2, None)
    l_1[...] = own1[B:]
    r_2[...] = own2[:B]
    out[:, :W] = jnp.concatenate([rotated(0, 0), own2[B:]], 0).T
    out[:, W:] = jnp.concatenate([own1[:B], rotated(3, 1)], 0).T

    @pl.when(flags[0] != 0)
    def _():
        l_0[...] = rotated(0, 1)

    @pl.when(flags[1] != 0)
    def _():
        r_3[...] = rotated(3, 0)


def edge_specs(chunk):
    return [
        pl.BlockSpec((B, chunk), lambda i, flags: (0, i * flags[0])),
        pl.BlockSpec((B, chunk), lambda i, flags: (0, i * flags[1])),
    ]


def final_inner(flags, y, pairs, chunk=2048):
    blocks = [x for pair in pairs for x in pair]
    cols = blocks[0].shape[1]
    spec = pl.BlockSpec((B, chunk), lambda i, flags: (0, i))
    block = jax.ShapeDtypeStruct((B, cols), F32)
    whole = pl.BlockSpec((PD, W, W), lambda i, flags: (0, 0, 0))
    return pl.pallas_call(
        final_inner_kernel,
        grid_spec=pltpu.PrefetchScalarGridSpec(
            num_scalar_prefetch=1,
            grid=(cols // chunk,),
            in_specs=[whole] + [spec] * len(blocks),
            out_specs=[pl.BlockSpec((chunk, 2 * W), lambda i, flags: (i, 0)), spec, spec]
            + edge_specs(chunk),
        ),
        out_shape=[jax.ShapeDtypeStruct((cols, 2 * W), F32)] + [block] * 4,
        compiler_params=params(),
        cost_estimate=LONG,
        name="final_inner",
    )(flags, y, *blocks)


def final_kernel(flags, y_left, y_right, lt, lb, rt, rb, l_1, r_2, l_0, r_3, inner, out):
    left = apply_rows(factor_stack(y_left[...]), jnp.concatenate([lt[...], lb[...]], 0))
    right = apply_rows(factor_stack(y_right[...]), jnp.concatenate([rt[...], rb[...]], 0))
    left = jnp.where(flags[0] != 0, l_0[...], left)
    right = jnp.where(flags[1] != 0, r_3[...], right)
    out[:, :W] = jnp.concatenate([left, l_1[...]], 0).T
    out[:, W : 3 * W] = inner[...]
    out[:, 3 * W :] = jnp.concatenate([r_2[...], right], 0).T


def final(flags, edges, left_pair, right_pair, done, inner, chunk=2048):
    cols = inner.shape[0]
    spec = pl.BlockSpec((B, chunk), lambda i, flags: (0, i))
    half = pl.BlockSpec((B, W), lambda i, flags: (0, 0))
    return pl.pallas_call(
        final_kernel,
        grid_spec=pltpu.PrefetchScalarGridSpec(
            num_scalar_prefetch=1,
            grid=(cols // chunk,),
            in_specs=[half, half]
            + [spec] * 6
            + edge_specs(chunk)
            + [pl.BlockSpec((chunk, 2 * W), lambda i, flags: (i, 0))],
            out_specs=pl.BlockSpec((chunk, PD * W), lambda i, flags: (i, 0)),
        ),
        out_shape=jax.ShapeDtypeStruct((cols, PD * W), F32),
        compiler_params=params(),
        cost_estimate=LONG,
        name="final",
    )(flags, *edges, *left_pair, *right_pair, *done, inner)


def send_on(x):
    peers = lax.axis_size("pair")
    return lax.ppermute(x, "pair", [(i, i + 1) for i in range(peers - 1)])


def send_back(x):
    peers = lax.axis_size("pair")
    return lax.ppermute(x, "pair", [(i + 1, i) for i in range(peers - 1)])


def after(x, *deps):
    return pl.pallas_call(
        lambda *refs: None,
        in_specs=[pl.BlockSpec(memory_space=pl.ANY)] * (1 + len(deps)),
        out_specs=pl.BlockSpec(memory_space=pl.ANY),
        out_shape=jax.ShapeDtypeStruct(x.shape, x.dtype),
        input_output_aliases={0: 0},
        cost_estimate=LONG,
        name="after",
    )(x, *deps)


def other_core(x):
    return lax.ppermute(x, "rows", [(i, i ^ 1) for i in range(4)])


def row_terms(mine, theirs):
    near = mine + other_core(theirs)
    return near, lax.ppermute(near, "rows", [(i, i ^ 2) for i in range(4)])


def body(matrix):
    index = lax.axis_index("pair")
    last = lax.axis_size("pair") - 1
    first_one, last_one = index == 0, index == last
    core = lax.axis_index("rows") % 2
    flags = jnp.stack([first_one, last_one, core]).astype(jnp.int32)

    near, far = row_terms(*gram_rows(matrix, "gram_1"))
    (y1,) = factors(flags, near, far, "factors_1")
    y1 = (y1, other_core(y1))
    r1_3, l1_0 = rotate_rows(flags, y1, [(3, 0), (0, 1)], matrix, "rotate_1_ends")
    in_left = send_on(r1_3)
    in_right = send_back(l1_0)
    r1_0, l1_3, r1_1, l1_1, r1_2, l1_2 = rotate_rows(
        flags, y1, [(0, 0), (3, 1), (1, None), (2, None)], matrix, "rotate_1_inner"
    )
    in_left2 = send_on(r1_2)

    in_left = jnp.where(first_one, l1_0, in_left)
    in_right = jnp.where(last_one, r1_3, in_right)
    pairs2 = [(in_left, l1_1), (r1_0, l1_2), (r1_1, l1_3), (r1_2, in_right)]
    near, far = row_terms(*[gram_blocks(pairs2, "gram_2")] * 2)
    l1_1 = after(l1_1, near, in_left2)
    pairs2[0] = (in_left, l1_1)
    in_right2 = send_back(l1_1)
    y2, to_left, to_right = factors(flags, near, far, "factors_2")
    edges2 = (send_on(to_right), send_back(to_left))
    r2_2, l2_1 = rotate_blocks(flags, (y2,), [(2, 0), (1, 1)], pairs2, "rotate_2_ends")
    in_left3 = send_on(r2_2)
    r2_left, r2_0, l2_0, r2_1, l2_2, r2_3, l2_3, l2_right, gram = round_2_rest(
        flags, y2, edges2, pairs2, (in_left2, l1_0), (r1_3, in_right2), (r2_2, l2_1)
    )

    pairs3 = [(r2_left, l2_1), (r2_0, l2_2), (r2_1, l2_3), (r2_2, l2_right)]
    near, far = row_terms(gram, gram)
    l2_1 = after(l2_1, near, in_left3)
    pairs3[0] = (r2_left, l2_1)
    in_right3 = send_back(l2_1)
    y3, to_left, to_right = factors(flags, near, far, "factors_3")
    edges3 = (send_on(to_right), send_back(to_left))
    inner, *done = final_inner(flags, y3, pairs3)
    return final(flags, edges3, (in_left3, l2_0), (r2_3, in_right3), done, inner)


def solution(mesh):
    spec = P("rows", "pair")
    return jax.shard_map(body, mesh=mesh, in_specs=(spec,), out_specs=spec, check_vma=False)
```
